256 devices in a mesh: seq: 32 (over z_hi, y, core), tp: 8 (over z_lo, x).
Axes of the slice: x: 4, y: 4, z: 8 (z_hi: 4, z_lo: 2; z = z_hi * 2 + z_lo), core: 2. Of those that a mesh axis runs over, the one named last changes fastest.
Arguments:
- sol_q: bfloat16 [8192, 5120], P('seq', 'tp')
- solution_keys: bfloat16 [8192, 1024], P('seq', 'tp')
- solution_values: bfloat16 [8192, 1024], P('seq', 'tp'), may hold values from -6 to 6
- crit_q: bfloat16 [64, 256, 5120], P('seq', None, 'tp')
- crit_k: bfloat16 [64, 256, 1024], P('seq', None, 'tp')
- critique_values: bfloat16 [64, 256, 1024], P('seq', None, 'tp'), may hold values from -6 to 6
- boundary: int32 [64], replicated, may hold values from 1 to 8192, as said below
- w_out: bfloat16 [5120, 5120], P('tp'), may hold values from -0.078125 to 0.078125
Outputs:
- sol_out: bfloat16 [8192, 5120], P('seq', 'tp')
- crit_out: bfloat16 [64, 256, 5120], P('seq', None, 'tp')
The draws below stay inside these ranges and needn't reach their ends.
Inputs may be any that keep to these rules, and one draw needn't show every extreme that they name: Strictly increasing over critiques; boundary[c] lies between c * 128 + 1 and (c + 1) * 128; the last one equals 8192.
All inputs are finite; a program needn't handle non-finite values.
Results may differ from the reference program's by a relative error of at most 0.02.
Values may be sent and summed in bfloat16 or wider, within the bound.
A program may use at most 128 MiB of HBM per device.

```python
import jax
import jax.numpy as jnp
from jax import lax

D = 5120
QUERY_HEADS = 40
KEY_VALUE_HEADS = 8
HEAD_WIDTH = 128
SOL_DEV = 256
CRITIQUE_LENGTH = 256
SOLUTION_LENGTH = 8192
CRITIQUE_COUNT = 64
N_TP = 8


def draw_solution_keys(key, part):
    key = jax.random.fold_in(key, 11)
    value_list = jax.random.normal(key, (SOLUTION_LENGTH, KEY_VALUE_HEADS * HEAD_WIDTH), jnp.float32)
    return value_list.astype(jnp.bfloat16)


def draw_sol_q(key, part):
    key = jax.random.fold_in(key, 12)
    value_list = jax.random.normal(key, (SOLUTION_LENGTH, QUERY_HEADS * HEAD_WIDTH), jnp.float32)
    return value_list.astype(jnp.bfloat16)


def draw_crit_k(key, part):
    key = jax.random.fold_in(key, 13)
    value_list = jax.random.normal(key, (CRITIQUE_COUNT, CRITIQUE_LENGTH, KEY_VALUE_HEADS * HEAD_WIDTH), jnp.float32)
    return value_list.astype(jnp.bfloat16)


def draw_crit_q(key, part):
    key = jax.random.fold_in(key, 14)
    value_list = jax.random.normal(key, (CRITIQUE_COUNT, CRITIQUE_LENGTH, QUERY_HEADS * HEAD_WIDTH), jnp.float32)
    return value_list.astype(jnp.bfloat16)


def draw_boundary(key, part):
    key = jax.random.fold_in(key, 17)
    spacing = SOLUTION_LENGTH // CRITIQUE_COUNT
    offsets = jax.random.randint(key, (CRITIQUE_COUNT,), 1, spacing + 1, jnp.int32)
    value_list = jnp.arange(CRITIQUE_COUNT, dtype=jnp.int32) * spacing + offsets
    return value_list.at[CRITIQUE_COUNT - 1].set(SOLUTION_LENGTH)


def block_levels(key, dims, cuts, low, high):
    level = 1.0
    for axis_at, shards_of in cuts:
        steps = jax.random.uniform(jax.random.fold_in(jax.random.fold_in(key, 6), axis_at), (shards_of,), jnp.float32, low / len(cuts), high / len(cuts))
        level = level * jnp.repeat(jnp.exp(steps), dims[axis_at] // shards_of).reshape((-1,) + (1,) * (len(dims) - 1 - axis_at))
    return level


def scatter_about(own_key, extent, width, most, cuts=(), held_as=jnp.bfloat16):
    values = jax.random.normal(own_key, extent, jnp.float32) * width
    if len(cuts) > 0:
        values = block_levels(own_key, extent, cuts, -0.22, 0.18) * values
    return jnp.clip(values, min=-most, max=most).astype(held_as)


def setup_inputs(seed: int = 0) -> dict:
    streams_of = jax.random.split(jax.random.key(seed), 9)
    return {
        "sol_q": draw_sol_q(jax.random.fold_in(streams_of[8], 71), 0),
        "solution_keys": draw_solution_keys(jax.random.fold_in(streams_of[8], 71), 0),
        "solution_values": scatter_about(streams_of[2], (SOLUTION_LENGTH, KEY_VALUE_HEADS * HEAD_WIDTH), 1.0, 6.0, ((0, 32), (1, 8))),
        "crit_q": draw_crit_q(jax.random.fold_in(streams_of[8], 71), 0),
        "crit_k": draw_crit_k(jax.random.fold_in(streams_of[8], 71), 0),
        "critique_values": scatter_about(streams_of[5], (CRITIQUE_COUNT, CRITIQUE_LENGTH, KEY_VALUE_HEADS * HEAD_WIDTH), 1.0, 6.0, ((0, 32), (2, 8))),
        "boundary": draw_boundary(jax.random.fold_in(streams_of[8], 71), 0),
        "w_out": scatter_about(streams_of[7], (QUERY_HEADS * HEAD_WIDTH, D), (QUERY_HEADS * HEAD_WIDTH) ** -0.5, 0.078125, ((0, 8),)),
    }


def attend_block(queries, key_list, value_list, allowed):
    scores = jnp.dot(queries, key_list.T, preferred_element_type=jnp.float32) * (HEAD_WIDTH ** -0.5)
    scores = jnp.where(allowed, scores, -1.0e30)
    highest = jnp.max(scores, axis=-1, keepdims=True)
    weights = jnp.exp(scores - highest)
    weight_sum = jnp.sum(weights, axis=-1, keepdims=True)
    numerator = jnp.dot(weights.astype(jnp.bfloat16), value_list, preferred_element_type=jnp.float32)
    return numerator / weight_sum


def solution_attention(sol_q, solution_keys, solution_values):
    group_length = QUERY_HEADS // KEY_VALUE_HEADS
    block_count = SOLUTION_LENGTH // SOL_DEV
    queries = sol_q.reshape(block_count, SOL_DEV, QUERY_HEADS, HEAD_WIDTH)
    key_list = solution_keys.reshape(SOLUTION_LENGTH, KEY_VALUE_HEADS, HEAD_WIDTH)
    value_list = solution_values.reshape(SOLUTION_LENGTH, KEY_VALUE_HEADS, HEAD_WIDTH)
    positions = jnp.arange(SOLUTION_LENGTH, dtype=jnp.int32)

    def one_head(head_index):
        head_keys = lax.dynamic_index_in_dim(key_list, head_index // group_length, 1, keepdims=False)
        head_values = lax.dynamic_index_in_dim(value_list, head_index // group_length, 1, keepdims=False)

        def one_block(block_index):
            block = lax.dynamic_index_in_dim(queries, block_index, 0, keepdims=False)
            block = lax.dynamic_index_in_dim(block, head_index, 1, keepdims=False)
            query_pos = block_index * SOL_DEV + jnp.arange(SOL_DEV, dtype=jnp.int32)
            allowed = positions[None, :] <= query_pos[:, None]
            return attend_block(block, head_keys, head_values, allowed)

        return lax.map(one_block, jnp.arange(block_count, dtype=jnp.int32))

    result = lax.map(one_head, jnp.arange(QUERY_HEADS, dtype=jnp.int32))
    return result.transpose(1, 2, 0, 3).reshape(SOLUTION_LENGTH, QUERY_HEADS * HEAD_WIDTH).astype(jnp.bfloat16)


def critique_attention(crit_q, crit_k, critique_values, solution_keys, solution_values, boundary):
    group_length = QUERY_HEADS // KEY_VALUE_HEADS
    key_pos = jnp.arange(SOLUTION_LENGTH + CRITIQUE_LENGTH, dtype=jnp.int32)
    token_pos = jnp.arange(CRITIQUE_LENGTH, dtype=jnp.int32)

    def one_critique(critique):
        queries = lax.dynamic_index_in_dim(crit_q, critique, 0, keepdims=False).reshape(CRITIQUE_LENGTH, QUERY_HEADS, HEAD_WIDTH)
        self_key_rows = lax.dynamic_index_in_dim(crit_k, critique, 0, keepdims=False)
        self_value_rows = lax.dynamic_index_in_dim(critique_values, critique, 0, keepdims=False)
        key_list = jnp.concatenate([solution_keys, self_key_rows], axis=0).reshape(SOLUTION_LENGTH + CRITIQUE_LENGTH, KEY_VALUE_HEADS, HEAD_WIDTH)
        value_list = jnp.concatenate([solution_values, self_value_rows], axis=0).reshape(SOLUTION_LENGTH + CRITIQUE_LENGTH, KEY_VALUE_HEADS, HEAD_WIDTH)
        boundary_at = lax.dynamic_index_in_dim(boundary, critique, 0, keepdims=False)
        allowed = jnp.where(key_pos[None, :] < SOLUTION_LENGTH, key_pos[None, :] < boundary_at,
                            (key_pos[None, :] - SOLUTION_LENGTH) <= token_pos[:, None])

        def one_head(head_index):
            head_queries = lax.dynamic_index_in_dim(queries, head_index, 1, keepdims=False)
            head_keys = lax.dynamic_index_in_dim(key_list, head_index // group_length, 1, keepdims=False)
            head_values = lax.dynamic_index_in_dim(value_list, head_index // group_length, 1, keepdims=False)
            return attend_block(head_queries, head_keys, head_values, allowed)

        result = lax.map(one_head, jnp.arange(QUERY_HEADS, dtype=jnp.int32))
        return result.transpose(1, 0, 2).reshape(CRITIQUE_LENGTH, QUERY_HEADS * HEAD_WIDTH).astype(jnp.bfloat16)

    return lax.map(one_critique, jnp.arange(CRITIQUE_COUNT, dtype=jnp.int32))


def project(attention, w_out):
    group_width = QUERY_HEADS * HEAD_WIDTH // N_TP
    summed = jnp.zeros((attention.shape[0], D), jnp.float32)
    for group_index in range(N_TP):
        partial_value = jnp.dot(attention[:, group_index * group_width:(group_index + 1) * group_width],
                          w_out[group_index * group_width:(group_index + 1) * group_width],
                          preferred_element_type=jnp.float32).astype(jnp.bfloat16)
        partial_value = lax.optimization_barrier(partial_value)
        summed = summed + partial_value.astype(jnp.float32)
    return summed.astype(jnp.bfloat16)


def reference(sol_q, solution_keys, solution_values, crit_q, crit_k, critique_values, boundary, w_out):
    sol_attention = solution_attention(sol_q, solution_keys, solution_values)
    crit_attention = critique_attention(crit_q, crit_k, critique_values, solution_keys, solution_values, boundary)
    sol_out = project(sol_attention, w_out)
    crit_out = project(crit_attention.reshape(CRITIQUE_COUNT * CRITIQUE_LENGTH, QUERY_HEADS * HEAD_WIDTH), w_out).reshape(CRITIQUE_COUNT, CRITIQUE_LENGTH, D)
    return sol_out, crit_out
```

```python
import functools
import math

import jax
import jax.numpy as jnp
from jax import lax
from jax.experimental import pallas as pl
from jax.experimental.pallas import tpu as pltpu
from jax.sharding import PartitionSpec as P

HEAD = 128
HEADS = 5
ROWS = 256
WIDE = HEADS * ROWS
COLS = HEADS * HEAD
KEYS = 512
NEG = -1e30
SCALE = math.log2(math.e) / math.sqrt(HEAD)
FUSED = True

ORDER = (
    (0, -1), (0, 1), (-1, 0), (1, 0), (0, 2), (2, 0), (-1, -1), (-1, 1),
    (1, -1), (1, 1), (-1, 2), (1, 2), (2, -1), (2, 1), (2, 2),
)
STEPS = (
    (("z", "m"), ("z", "p"), ("y", "0", "m"), ("y", "0", "p")),
    (("z", "2"),),
    (("y", "0", "2"),),
    (("y", "m", "m"),),
    (("y", "m", "p"),),
    (("y", "p", "m"), ("y", "p", "p")),
    (("y", "m", "2"),),
    (("y", "p", "2"),),
    (("y", "2", "m"),),
    (("y", "2", "p"),),
    (("y", "2", "2"),),
    (), (), (), (),
)


def pick(index, table):
    value = jnp.int32(table[0])
    for at, entry in enumerate(table[1:], 1):
        value = jnp.where(index == at, jnp.int32(entry), value)
    return value


def kernel(
    sol_q, sol_k, sol_v, crit_q, crit_k, crit_v, bnd, w_hbm, out,
    kv, own_kv, sbuf, acc, top, att, w2, relay, psend, precv, pown,
    kv_send, kv_recv, w_send, w_recv, wl_sem, x_send, x_recv, p_send, p_recv,
):
    s = lax.axis_index("seq")
    t = lax.axis_index("tp")
    a, b, c = s // 8, (s // 2) % 4, s % 2
    ch = s // 2
    sib = s + 1 - 2 * c
    zl, x = t // 4, t % 4
    d = 1 - 2 * c

    def seq_at(za, yb):
        return za * 8 + yb * 2 + c

    def hop(v, by):
        return (v + by + 8) % 4

    def rel(v, which):
        return {"0": v, "m": hop(v, -d), "p": hop(v, d), "2": hop(v, 2)}[which]

    def tp_at(xx):
        return zl * 4 + xx

    partner = (1 - zl) * 4 + x

    def remote(src, dst, ssem, rsem, seq=None, tp=None):
        return pltpu.make_async_remote_copy(
            src_ref=src, dst_ref=dst, send_sem=ssem, recv_sem=rsem,
            device_id={"seq": s if seq is None else seq, "tp": t if tp is None else tp},
            device_id_type=pl.DeviceIdType.MESH,
        )

    kv[s, 0:256, :] = sol_k[...]
    kv[s, 256:384, :] = sol_v[0:128, :].T
    kv[s, 384:512, :] = sol_v[128:256, :].T
    for i in range(2):
        own_kv[i, 0:256, :] = crit_k[i]
        own_kv[i, 256:384, :] = crit_v[i, 0:128, :].T
        own_kv[i, 384:512, :] = crit_v[i, 128:256, :].T

    barrier = pltpu.get_barrier_semaphore()
    friends = [
        (seq_at(hop(a, 1), b), t), (seq_at(hop(a, -1), b), t),
        (seq_at(a, hop(b, 1)), t), (seq_at(a, hop(b, -1)), t), (sib, t),
    ]
    if FUSED:
        friends += [(s, tp_at(hop(x, 1))), (s, tp_at(hop(x, -1))), (s, partner)]
    for fs, ft in friends:
        pl.semaphore_signal(
            barrier, inc=1, device_id={"seq": fs, "tp": ft}, device_id_type=pl.DeviceIdType.MESH
        )
    pl.semaphore_wait(barrier, len(friends))

    sent = [0]

    def send_kv(block, to):
        k = sent[0]
        sent[0] += 1
        remote(kv.at[block], kv.at[block], kv_send.at[k], kv_recv.at[block], seq=to).start()

    def wait_kv(block):
        remote(kv.at[block], kv.at[block], kv_send.at[0], kv_recv.at[block], seq=sib).wait_recv()

    def send_y(block):
        send_kv(block, seq_at(a, hop(b, d)))
        send_kv(block, seq_at(a, hop(b, -d)))

    send_kv(s, seq_at(hop(a, d), b))
    send_kv(s, seq_at(hop(a, -d), b))
    send_y(s)
    send_kv(s, sib)

    def service(item):
        if item[0] == "z":
            block = seq_at(rel(a, item[1]), b)
            wait_kv(block)
            if item[1] == "m":
                send_kv(block, seq_at(hop(a, d), b))
            send_y(block)
            send_kv(block, sib)
        else:
            block = seq_at(rel(a, item[1]), rel(b, item[2]))
            wait_kv(block)
            if item[2] == "m":
                send_kv(block, seq_at(a, hop(b, d)))
            send_kv(block, sib)

    def w_from(rows, count, group):
        return w_hbm.at[pl.ds(rows, count), pl.ds(pl.multiple_of(group * COLS, 128), COLS)]

    half = pl.multiple_of(c * 320, 16)

    def w_part(owner, which_half):
        return w2.at[owner, :, pl.ds(pl.multiple_of(which_half * 320, 16), 320), :]

    if FUSED:
        for i in range(2):
            remote(
                w_from(half, 320, i * 4 + hop(x, 2)), relay.at[i],
                w_send.at[i], w_recv.at[i], tp=tp_at(hop(x, d)),
            ).start()
        for n, by in enumerate((d, -d)):
            for i in range(2):
                remote(
                    w_from(half, 320, i * 4 + hop(x, by)),
                    w2.at[x, i, pl.ds(half, 320), :],
                    w_send.at[2 + n * 2 + i], w_recv.at[2 + n * 2 + i], tp=tp_at(hop(x, by)),
                ).start()
        for i in range(2):
            pltpu.make_async_copy(w_from(0, COLS, i * 4 + x), w2.at[x, i], wl_sem.at[i]).start()

    def w_forward():
        for i in range(2):
            remote(
                relay.at[i], relay.at[i], w_send.at[0], w_recv.at[i], tp=tp_at(hop(x, d))
            ).wait_recv()
        remote(
            relay, w_part(hop(x, -d), c), w_send.at[6], w_recv.at[6], tp=tp_at(hop(x, d))
        ).start()

    def w_share_near():
        for n, by in enumerate((-d, d)):
            owner = hop(x, by)
            for i in range(2):
                ref = w2.at[owner, i, pl.ds(half, 320), :]
                remote(
                    ref, ref, w_send.at[0], w_recv.at[2 + n * 2 + i], tp=tp_at(owner)
                ).wait_recv()
            remote(
                w_part(owner, c), w_part(owner, c), w_send.at[7 + n], w_recv.at[7 + n], seq=sib
            ).start()

    def w_share_far():
        owner = hop(x, 2)
        ref = w_part(owner, c)
        remote(ref, ref, w_send.at[0], w_recv.at[6], tp=tp_at(hop(x, d))).wait_recv()
        remote(ref, ref, w_send.at[9], w_recv.at[9], seq=sib).start()

    def w_ready():
        for n, by in enumerate((d, -d)):
            ref = w_part(hop(x, by), 1 - c)
            remote(ref, ref, w_send.at[0], w_recv.at[7 + n], seq=sib).wait_recv()
        ref = w_part(hop(x, 2), 1 - c)
        remote(ref, ref, w_send.at[0], w_recv.at[9], seq=sib).wait_recv()
        for i in range(2):
            pltpu.make_async_copy(w_from(0, COLS, i * 4 + x), w2.at[x, i], wl_sem.at[i]).wait()

    def query(g, h):
        if isinstance(g, int) and g == 0:
            return sol_q[:, h * HEAD:(h + 1) * HEAD]
        return crit_q[g - 1, :, h * HEAD:(h + 1) * HEAD]

    def dot_keys(keys, g, h):
        return lax.dot_general(
            keys, query(g, h), (((1,), (1,)), ((), ())), preferred_element_type=jnp.float32
        )

    def keys_of(j):
        return kv[pl.ds(2 * j, 2), 0:256, :].reshape(KEYS, HEAD)

    def values_of(j):
        parts = [kv[2 * j, 256:384, :], kv[2 * j, 384:512, :],
                 kv[2 * j + 1, 256:384, :], kv[2 * j + 1, 384:512, :]]
        return jnp.concatenate(
            [jnp.concatenate(parts, axis=1), jnp.ones((16, KEYS), jnp.bfloat16)], axis=0
        )

    def absorb(h, scores, values):
        cs = slice(h * ROWS, (h + 1) * ROWS)
        old = top[0:1, cs]
        new = jnp.maximum(old, jnp.max(scores, axis=0, keepdims=True))
        rescale = jnp.exp2((old - new) * SCALE)
        weights = jnp.exp2((scores - new) * SCALE).astype(jnp.bfloat16)
        acc[:, cs] = acc[:, cs] * rescale + lax.dot_general(
            values, weights, (((1,), (0,)), ((), ())), preferred_element_type=jnp.float32
        )
        top[0:1, cs] = new

    def begin(g):
        top[...] = jnp.full_like(top, NEG)
        acc[...] = jnp.zeros_like(acc)
        keys = keys_of(ch)
        key_at = lax.broadcasted_iota(jnp.int32, (KEYS, ROWS), 0)
        if isinstance(g, int) and g == 0:
            allowed = key_at <= lax.broadcasted_iota(jnp.int32, (KEYS, ROWS), 1) + 256 * c
        else:
            allowed = key_at < bnd[2 * s + g - 1] - KEYS * ch
        for h in range(HEADS):
            sbuf[h] = jnp.where(allowed, dot_keys(keys, g, h), NEG)

    def advance(g, now, then):
        values, keys = values_of(now), keys_of(then)
        for h in range(HEADS):
            absorb(h, sbuf[h], values)
            sbuf[h] = dot_keys(keys, g, h)

    def only_keys(g, then):
        keys = keys_of(then)
        for h in range(HEADS):
            sbuf[h] = dot_keys(keys, g, h)

    def last(now):
        values = values_of(now)
        for h in range(HEADS):
            absorb(h, sbuf[h], values)

    def finish(g):
        for h in range(HEADS):
            cs = slice(h * ROWS, (h + 1) * ROWS)
            value = acc[0:HEAD, cs] * (1.0 / acc[HEAD:HEAD + 1, cs])
            att[g, x, :, h * HEAD:(h + 1) * HEAD] = value.T.astype(jnp.bfloat16)

    def x_start(g):
        ref = att.at[g, x]
        remote(ref, ref, x_send.at[3 * g], x_recv.at[4 * g + x], tp=tp_at(hop(x, d))).start()
        remote(ref, ref, x_send.at[3 * g + 1], x_recv.at[4 * g + x], tp=tp_at(hop(x, -d))).start()

    def x_wait(g, owner):
        ref = att.at[g, owner]
        remote(ref, ref, x_send.at[0], x_recv.at[4 * g + owner], tp=tp_at(hop(x, d))).wait_recv()

    def x_forward(g):
        owner = hop(x, -d)
        x_wait(g, owner)
        ref = att.at[g, owner]
        remote(
            ref, ref, x_send.at[3 * g + 2], x_recv.at[4 * g + owner], tp=tp_at(hop(x, d))
        ).start()

    def project(g):
        x_wait(g, hop(x, d))
        x_wait(g, hop(x, 2))
        for mine in (False, True):
            z = zl if mine else 1 - zl
            total = jnp.zeros((ROWS, COLS), jnp.float32)
            for o in range(4):
                total += jnp.dot(att[g, o], w2[o, z], preferred_element_type=jnp.float32)
            if mine:
                pown[g] = total
            else:
                psend[g] = total.astype(jnp.bfloat16)
                remote(
                    psend.at[g], precv.at[g], p_send.at[g], p_recv.at[g], tp=partner
                ).start()

    def complete(g):
        remote(psend.at[g], precv.at[g], p_send.at[g], p_recv.at[g], tp=partner).wait_recv()
        out[g] = (pown[g] + precv[g].astype(jnp.float32)).astype(jnp.bfloat16)

    wait_kv(sib)
    begin(0)

    def slot(e, carry):
        before, before_ok = carry
        for at, items in enumerate(STEPS):
            if items:
                @pl.when(e == at)
                def _(items=items):
                    for item in items:
                        service(item)
        j = hop(a, pick(e, [o[0] for o in ORDER])) * 4 + hop(b, pick(e, [o[1] for o in ORDER]))
        wait_kv(2 * j + 1 - c)
        ok = j < ch

        @pl.when(before_ok)
        def _():
            advance(0, before, j)

        @pl.when(jnp.logical_and(jnp.logical_not(before_ok), ok))
        def _():
            only_keys(0, j)

        return j, ok

    before, before_ok = lax.fori_loop(0, 15, slot, (ch, jnp.bool_(True)))

    @pl.when(before_ok)
    def _():
        last(before)

    finish(0)
    if FUSED:
        x_start(0)
        w_forward()

    def group(g, _):
        begin(g)

        def step(i, _):
            if FUSED:
                @pl.when(i == 4)
                def _():
                    x_forward(g - 1)

                @pl.when(jnp.logical_and(i == 5, g == 1))
                def _():
                    w_share_near()

                @pl.when(jnp.logical_and(i == 11, g == 1))
                def _():
                    w_share_far()
            advance(g, jnp.where(i == 0, ch, i - 1), i)
            return 0

        lax.fori_loop(0, ch, step, 0)
        last(jnp.where(ch == 0, ch, ch - 1))
        keys = own_kv[g - 1, 0:256, :]
        values = jnp.concatenate(
            [
                jnp.concatenate([own_kv[g - 1, 256:384, :], own_kv[g - 1, 384:512, :]], axis=1),
                jnp.ones((16, 256), jnp.bfloat16),
            ],
            axis=0,
        )
        shape = (256, ROWS)
        allowed = lax.broadcasted_iota(jnp.int32, shape, 0) <= lax.broadcasted_iota(jnp.int32, shape, 1)
        for h in range(HEADS):
            sbuf[h, 0:256, :] = jnp.where(allowed, dot_keys(keys, g, h), NEG)
        for h in range(HEADS):
            absorb(h, sbuf[h, 0:256, :], values)
        finish(g)
        if FUSED:
            x_start(g)

            @pl.when(ch <= 4)
            def _():
                x_forward(g - 1)

            @pl.when(g == 1)
            def _():
                @pl.when(ch <= 5)
                def _():
                    w_share_near()

                @pl.when(ch <= 11)
                def _():
                    w_share_far()

                w_ready()

            project(g - 1)
        return 0

    lax.fori_loop(1, 3, group, 0)
    if FUSED:
        x_forward(2)
        complete(0)
        complete(1)
        project(2)
        complete(2)
    else:
        for g in range(3):
            out[g] = att[g, x]

    for k in range(sent[0]):
        remote(kv.at[0], kv.at[0], kv_send.at[k], kv_recv.at[0], seq=sib).wait_send()
    if FUSED:
        for i in range(6):
            remote(relay.at[0], relay.at[0], w_send.at[i], w_recv.at[0], tp=partner).wait_send()
        for i in range(6, 10):
            remote(relay, relay, w_send.at[i], w_recv.at[0], tp=partner).wait_send()
        for i in range(9):
            ref = att.at[0, 0]
            remote(ref, ref, x_send.at[i], x_recv.at[0], tp=partner).wait_send()
        for g in range(3):
            remote(psend.at[g], precv.at[g], p_send.at[g], p_recv.at[g], tp=partner).wait_send()


def per_device(
    sol_q, solution_keys, solution_values, crit_q, crit_k, critique_values, boundary, w_out
):
    vmem = pl.BlockSpec(memory_space=pltpu.VMEM)
    bf, f32 = jnp.bfloat16, jnp.float32
    dma = pltpu.SemaphoreType.DMA
    result = pl.pallas_call(
        kernel,
        out_shape=jax.ShapeDtypeStruct((3, ROWS, COLS), bf),
        in_specs=[vmem] * 6 + [pl.BlockSpec(memory_space=pltpu.SMEM), pl.BlockSpec(memory_space=pl.ANY)],
        out_specs=vmem,
        scratch_shapes=[
            pltpu.VMEM((32, 512, HEAD), bf),
            pltpu.VMEM((2, 512, HEAD), bf),
            pltpu.VMEM((HEADS, KEYS, ROWS), f32),
            pltpu.VMEM((HEAD + 16, WIDE), f32),
            pltpu.VMEM((8, WIDE), f32),
            pltpu.VMEM((3, 4, ROWS, COLS), bf),
            pltpu.VMEM((4, 2, COLS, COLS), bf),
            pltpu.VMEM((2, 320, COLS), bf),
            pltpu.VMEM((3, ROWS, COLS), bf),
            pltpu.VMEM((3, ROWS, COLS), bf),
            pltpu.VMEM((3, ROWS, COLS), f32),
            dma((31,)), dma((32,)), dma((10,)), dma((10,)), dma((2,)),
            dma((9,)), dma((12,)), dma((3,)), dma((3,)),
        ],
        compiler_params=pltpu.CompilerParams(
            collective_id=0, has_side_effects=True, vmem_limit_bytes=50 * 2**20
        ),
        cost_estimate=pl.CostEstimate(
            flops=20_000_000_000, bytes_accessed=16_000_000, transcendentals=32_000_000
        ),
    )(sol_q, solution_keys, solution_values, crit_q, crit_k, critique_values, boundary, w_out)
    if not FUSED:
        partial = jnp.dot(result.reshape(768, COLS), w_out, preferred_element_type=f32)
        result = lax.psum_scatter(
            partial.astype(bf), "tp", scatter_dimension=1, tiled=True
        ).reshape(3, ROWS, COLS)
    return result[0], result[1:]


def solution(mesh):
    in_specs = (
        P("seq", "tp"), P("seq", "tp"), P("seq", "tp"),
        P("seq", None, "tp"), P("seq", None, "tp"), P("seq", None, "tp"),
        P(), P("tp", None),
    )
    out_specs = (P("seq", "tp"), P("seq", None, "tp"))
    return jax.shard_map(
        per_device, mesh=mesh, in_specs=in_specs, out_specs=out_specs, check_vma=False
    )
```

```python
import functools
import math

import jax
import jax.numpy as jnp
from jax import lax
from jax.experimental import pallas as pl
from jax.experimental.pallas import tpu as pltpu
from jax.sharding import PartitionSpec as P

HEAD = 128
HEADS = 5
ROWS = 256
WIDE = HEADS * ROWS
COLS = HEADS * HEAD
KEYS = 512
NEG = -1e30
SCALE = math.log2(math.e) / math.sqrt(HEAD)
VMEM_LIMIT = 63 * 2**20
KV = True
ATT = True
WX = True
XX = True
PJ = True

ORDER = (
    (0, -1), (0, 1), (-1, 0), (1, 0), (0, 2), (2, 0), (-1, -1), (-1, 1),
    (1, -1), (1, 1), (-1, 2), (1, 2), (2, -1), (2, 1), (2, 2),
)
STEPS = (
    (("y", "0", "m"), ("z", "m"), ("z", "p"), ("y", "0", "p")),
    (),
    (("y", "0", "2"),),
    (("z", "2"), ("w",)),
    (),
    (("y", "m", "m"), ("y", "p", "m")),
    (("y", "m", "p"), ("y", "p", "p")),
    (),
    (("y", "2", "m"),),
    (("y", "2", "p"),),
    (("y", "m", "2"), ("y", "p", "2")),
    (("y", "2", "2"),),
    (), (), (),
)


def pick(index, table):
    value = jnp.int32(table[0])
    for at, entry in enumerate(table[1:], 1):
        value = jnp.where(index == at, jnp.int32(entry), value)
    return value


def kernel(
    sol_q_in, sol_k_in, sol_v_in, crit_q_in, crit_k_in, crit_v_in, bnd_in, w_hbm, sol_out, crit_out,
    sol_q, sol_k, sol_v, crit_q, crit_k, crit_v, bnd, kv, own_kv, sbuf, acc, top, att, wown, wpar,
    hold, msend, mrecv, done,
    in_sem, out_sem, kv_send, kv_recv, w_send, w_recv, z_send, z_recv, m_send, m_recv,
):
    s = lax.axis_index("seq")
    t = lax.axis_index("tp")
    a, b, c = s // 8, (s // 2) % 4, s % 2
    ch = s // 2
    sib = s + 1 - 2 * c
    zl, x = t // 4, t % 4
    d = 1 - 2 * c

    def seq_at(za, yb):
        return za * 8 + yb * 2 + c

    def hop(v, by):
        return (v + by + 8) % 4

    def rel(v, which):
        return {"0": v, "m": hop(v, -d), "p": hop(v, d), "2": hop(v, 2)}[which]

    def tp_at(xx):
        return zl * 4 + xx

    partner = (1 - zl) * 4 + x
    beyond = seq_at(hop(a, 2 * zl - 1), b)

    def remote(src, dst, ssem, rsem, seq=None, tp=None):
        return pltpu.make_async_remote_copy(
            src_ref=src, dst_ref=dst, send_sem=ssem, recv_sem=rsem,
            device_id={"seq": s if seq is None else seq, "tp": t if tp is None else tp},
            device_id_type=pl.DeviceIdType.MESH,
        )

    loads = [
        pltpu.make_async_copy(src, dst, in_sem.at[k])
        for k, (src, dst) in enumerate((
            (sol_k_in, sol_k), (sol_v_in, sol_v), (sol_q_in, sol_q), (crit_k_in, crit_k),
            (crit_v_in, crit_v), (crit_q_in, crit_q), (bnd_in, bnd),
            (w_hbm.at[:, pl.ds(pl.multiple_of(zl * 2560, 128), 2560)], wown),
        ))
    ]
    for load in loads:
        load.start()

    barrier = pltpu.get_barrier_semaphore()
    friends = [
        (seq_at(hop(a, 1), b), t), (seq_at(hop(a, -1), b), t),
        (seq_at(a, hop(b, 1)), t), (seq_at(a, hop(b, -1)), t), (sib, t),
    ]
    friends += [(s, tp_at(hop(x, 1))), (s, tp_at(hop(x, -1))), (s, partner), (beyond, partner)]
    for fs, ft in friends:
        pl.semaphore_signal(
            barrier, inc=1, device_id={"seq": fs, "tp": ft}, device_id_type=pl.DeviceIdType.MESH
        )
    loads[0].wait()
    loads[1].wait()
    kv[s, 0:256, :] = sol_k[...]
    kv[s, 256:384, :] = sol_v[0:128, :].T
    kv[s, 384:512, :] = sol_v[128:256, :].T
    pl.semaphore_wait(barrier, len(friends))

    sent = [0]

    def send_kv(block, to):
        if not KV:
            return
        k = sent[0]
        sent[0] += 1
        remote(kv.at[block], kv.at[block], kv_send.at[k], kv_recv.at[block], seq=to).start()

    def wait_kv(block):
        if not KV:
            return
        remote(kv.at[block], kv.at[block], kv_send.at[0], kv_recv.at[block], seq=sib).wait_recv()

    def send_y(block):
        send_kv(block, seq_at(a, hop(b, d)))
        send_kv(block, seq_at(a, hop(b, -d)))

    send_kv(s, seq_at(hop(a, d), b))
    send_kv(s, seq_at(hop(a, -d), b))
    send_y(s)
    send_kv(s, sib)

    def service(item):
        if item[0] == "w":
            w_start()
            return
        if item[0] == "z":
            block = seq_at(rel(a, item[1]), b)
            wait_kv(block)
            if item[1] == "m":
                send_kv(block, seq_at(hop(a, d), b))
            send_y(block)
            send_kv(block, sib)
        else:
            block = seq_at(rel(a, item[1]), rel(b, item[2]))
            wait_kv(block)
            if item[2] == "m":
                send_kv(block, seq_at(a, hop(b, d)))
            send_kv(block, sib)

    def w_copy(n):
        rows = pl.ds(pl.multiple_of(c * 320 + n * 160, 16), 160)
        return remote(
            w_hbm.at[rows, pl.ds(pl.multiple_of((1 - zl) * 2560, 128), 2560)],
            wpar.at[rows, :], w_send.at[n], w_recv.at[n],
            seq=(s, beyond)[n], tp=partner,
        )

    def w_start():
        if WX:
            w_copy(0).start()
            w_copy(1).start()

    def w_shared(which):
        rows = pl.ds(pl.multiple_of(which * 320, 16), 320)
        return remote(wpar.at[rows, :], wpar.at[rows, :], w_send.at[2], w_recv.at[2], seq=sib)

    def w_share():
        if WX:
            w_copy(0).wait_recv()
            w_copy(1).wait_recv()
            w_shared(c).start()

    def w_ready():
        if WX:
            w_shared(1 - c).wait_recv()
        loads[7].wait()

    def query(g, h):
        if isinstance(g, int) and g == 0:
            return sol_q[:, h * HEAD:(h + 1) * HEAD]
        return crit_q[g - 1, :, h * HEAD:(h + 1) * HEAD]

    def dot_keys(keys, g, h):
        return lax.dot_general(
            keys, query(g, h), (((1,), (1,)), ((), ())), preferred_element_type=jnp.float32
        )

    def keys_of(j):
        return kv[pl.ds(2 * j, 2), 0:256, :].reshape(KEYS, HEAD)

    def values_of(j):
        parts = [kv[2 * j, 256:384, :], kv[2 * j, 384:512, :],
                 kv[2 * j + 1, 256:384, :], kv[2 * j + 1, 384:512, :]]
        return jnp.concatenate(
            [jnp.concatenate(parts, axis=1), jnp.ones((16, KEYS), jnp.bfloat16)], axis=0
        )

    def absorb(u, h, scores, values):
        cs = slice(h * ROWS, (h + 1) * ROWS)
        old = top[u, 0:1, cs]
        new = jnp.maximum(old, jnp.max(scores, axis=0, keepdims=True))
        rescale = jnp.exp2((old - new) * SCALE)
        weights = jnp.exp2((scores - new) * SCALE).astype(jnp.bfloat16)
        acc[u, :, cs] = acc[u, :, cs] * rescale + lax.dot_general(
            values, weights, (((1,), (0,)), ((), ())), preferred_element_type=jnp.float32
        )
        top[u, 0:1, cs] = new

    def begin(u, g):
        if not ATT:
            return
        top[u] = jnp.full((8, WIDE), NEG, jnp.float32)
        acc[u] = jnp.zeros((HEAD + 16, WIDE), jnp.float32)
        keys = keys_of(ch)
        key_at = lax.broadcasted_iota(jnp.int32, (KEYS, ROWS), 0)
        if g == 0:
            allowed = key_at <= lax.broadcasted_iota(jnp.int32, (KEYS, ROWS), 1) + 256 * c
        else:
            allowed = key_at < bnd[2 * s + g - 1] - KEYS * ch
        for h in range(HEADS):
            sbuf[u, h] = jnp.where(allowed, dot_keys(keys, g, h), NEG)

    def advance(units, now, then):
        if not ATT:
            return
        values, keys = values_of(now), keys_of(then)
        for h in range(HEADS):
            for u, g in units:
                absorb(u, h, sbuf[u, h], values)
                sbuf[u, h] = dot_keys(keys, g, h)

    def only_keys(units, then):
        if not ATT:
            return
        keys = keys_of(then)
        for h in range(HEADS):
            for u, g in units:
                sbuf[u, h] = dot_keys(keys, g, h)

    def last(units, now):
        if not ATT:
            return
        values = values_of(now)
        for h in range(HEADS):
            for u, g in units:
                absorb(u, h, sbuf[u, h], values)

    def own(u, g):
        if not ATT:
            return
        keys = own_kv[g - 1, 0:256, :]
        values = jnp.concatenate(
            [
                jnp.concatenate([own_kv[g - 1, 256:384, :], own_kv[g - 1, 384:512, :]], axis=1),
                jnp.ones((16, 256), jnp.bfloat16),
            ],
            axis=0,
        )
        shape = (256, ROWS)
        allowed = lax.broadcasted_iota(jnp.int32, shape, 0) <= lax.broadcasted_iota(jnp.int32, shape, 1)
        for h in range(HEADS):
            sbuf[u, h, 0:256, :] = jnp.where(allowed, dot_keys(keys, g, h), NEG)
        for h in range(HEADS):
            absorb(u, h, sbuf[u, h, 0:256, :], values)

    def finish(u, g):
        if not ATT:
            return
        for h in range(HEADS):
            cs = slice(h * ROWS, (h + 1) * ROWS)
            value = acc[u, 0:HEAD, cs] * (1.0 / acc[u, HEAD:HEAD + 1, cs])
            att[g, 0, :, h * HEAD:(h + 1) * HEAD] = value.astype(jnp.bfloat16).T

    def z_copy(chunk):
        k, g, r, n = chunk
        return remote(
            att.at[g, 0, pl.ds(r, n), :], att.at[g, 1, pl.ds(r, n), :],
            z_send.at[k], z_recv.at[k], tp=partner,
        )

    def m_copy(chunk, kind, to):
        k, g, r, n = chunk
        return remote(
            msend.at[g, kind, pl.ds(r, n), :], mrecv.at[g, kind, pl.ds(r, n), :],
            m_send.at[3 * k + kind], m_recv.at[3 * k + kind], tp=tp_at(to),
        )

    def z_start(chunk):
        if XX:
            z_copy(chunk).start()

    def project(chunk):
        k, g, r, n = chunk
        if XX:
            z_copy(chunk).wait_recv()

        def part(at):
            cols = pl.ds(pl.multiple_of(at * COLS, 128), COLS)
            if not PJ:
                return jnp.zeros((n, COLS), jnp.float32)
            return jnp.dot(
                att[g, 0, r:r + n, :], wown[:, cols], preferred_element_type=jnp.float32
            ) + jnp.dot(att[g, 1, r:r + n, :], wpar[:, cols], preferred_element_type=jnp.float32)

        for kind, at, to in ((0, hop(x, 2), hop(x, d)), (1, hop(x, -d), hop(x, -d))):
            msend[g, kind, r:r + n, :] = part(at).astype(jnp.bfloat16)
            if XX:
                m_copy(chunk, kind, to).start()
        hold[g, 0, r:r + n, :] = part(hop(x, d))
        hold[g, 1, r:r + n, :] = part(x)

    def relay(chunk):
        k, g, r, n = chunk
        if XX:
            m_copy(chunk, 0, hop(x, d)).wait_recv()
        total = hold[g, 0, r:r + n, :] + mrecv[g, 0, r:r + n, :].astype(jnp.float32)
        msend[g, 2, r:r + n, :] = total.astype(jnp.bfloat16)
        if XX:
            m_copy(chunk, 2, hop(x, d)).start()

    def store(chunk):
        k, g, r, n = chunk
        rows = pl.ds(r, n)
        ref = sol_out.at[rows, :] if g == 0 else crit_out.at[g - 1, rows, :]
        return pltpu.make_async_copy(done.at[g, rows, :], ref, out_sem.at[k])

    def complete(chunk):
        k, g, r, n = chunk
        total = hold[g, 1, r:r + n, :]
        for kind in (1, 2):
            if XX:
                m_copy(chunk, kind, hop(x, d)).wait_recv()
            total += mrecv[g, kind, r:r + n, :].astype(jnp.float32)
        done[g, r:r + n, :] = total.astype(jnp.bfloat16)
        store(chunk).start()

    chunks = ((0, 0, 0, 256), (1, 1, 0, 256), (2, 2, 0, 128), (3, 2, 128, 128))

    wait_kv(sib)
    for k in (2, 3, 4, 5, 6):
        loads[k].wait()
    for i in range(2):
        own_kv[i, 0:256, :] = crit_k[i]
        own_kv[i, 256:384, :] = crit_v[i, 0:128, :].T
        own_kv[i, 384:512, :] = crit_v[i, 128:256, :].T
    first = ((0, 0), (1, 1))
    begin(0, 0)
    begin(1, 1)

    def slot(e, carry):
        before, before_ok = carry
        for at, items in enumerate(STEPS):
            if items:
                @pl.when(e == at)
                def _(items=items):
                    for item in items:
                        service(item)
        j = hop(a, pick(e, [o[0] for o in ORDER])) * 4 + hop(b, pick(e, [o[1] for o in ORDER]))
        wait_kv(2 * j + 1 - c)
        ok = j < ch

        @pl.when(before_ok)
        def _():
            advance(first, before, j)

        @pl.when(jnp.logical_and(jnp.logical_not(before_ok), ok))
        def _():
            only_keys(first, j)

        return j, ok

    before, before_ok = lax.fori_loop(0, 15, slot, (ch, jnp.bool_(True)))

    @pl.when(before_ok)
    def _():
        last(first, before)

    finish(0, 0)
    z_start(chunks[0])
    own(1, 1)
    finish(1, 1)

    begin(0, 2)
    second = ((0, 2),)

    def step(i, _):
        for at, work in (
            (1, w_share),
            (2, lambda: z_start(chunks[1])),
            (5, lambda: (w_ready(), project(chunks[0]))),
            (9, lambda: (project(chunks[1]), relay(chunks[0]))),
            (14, lambda: relay(chunks[1])),
        ):
            @pl.when(i == at)
            def _(work=work):
                work()

        @pl.when(i < ch)
        def _():
            advance(second, jnp.where(i == 0, ch, i - 1), i)

        return 0

    lax.fori_loop(0, 15, step, 0)
    last(second, jnp.where(ch == 0, ch, ch - 1))
    own(0, 2)
    finish(0, 2)
    z_start(chunks[2])
    z_start(chunks[3])
    complete(chunks[0])
    project(chunks[2])
    project(chunks[3])
    relay(chunks[2])
    complete(chunks[1])
    relay(chunks[3])
    complete(chunks[2])
    complete(chunks[3])

    for k in range(sent[0]):
        remote(kv.at[0], kv.at[0], kv_send.at[k], kv_recv.at[0], seq=sib).wait_send()
    if WX:
        w_copy(0).wait_send()
        w_copy(1).wait_send()
        w_shared(c).wait_send()
    for chunk in chunks:
        if XX:
            z_copy(chunk).wait_send()
            for kind in range(3):
                m_copy(chunk, kind, hop(x, d)).wait_send()
        store(chunk).wait()


def per_device(
    sol_q, solution_keys, solution_values, crit_q, crit_k, critique_values, boundary, w_out
):
    bf, f32 = jnp.bfloat16, jnp.float32
    dma = pltpu.SemaphoreType.DMA
    hbm = pl.BlockSpec(memory_space=pl.ANY)
    sol_out, crit_out = pl.pallas_call(
        kernel,
        out_shape=(
            jax.ShapeDtypeStruct((ROWS, COLS), bf), jax.ShapeDtypeStruct((2, ROWS, COLS), bf)
        ),
        in_specs=[hbm] * 8,
        out_specs=(hbm, hbm),
        scratch_shapes=[
            pltpu.VMEM((ROWS, COLS), bf),
            pltpu.VMEM((ROWS, HEAD), bf),
            pltpu.VMEM((ROWS, HEAD), bf),
            pltpu.VMEM((2, ROWS, COLS), bf),
            pltpu.VMEM((2, ROWS, HEAD), bf),
            pltpu.VMEM((2, ROWS, HEAD), bf),
            pltpu.SMEM((64,), jnp.int32),
            pltpu.VMEM((32, 512, HEAD), bf),
            pltpu.VMEM((2, 512, HEAD), bf),
            pltpu.VMEM((2, HEADS, KEYS, ROWS), f32),
            pltpu.VMEM((2, HEAD + 16, WIDE), f32),
            pltpu.VMEM((2, 8, WIDE), f32),
            pltpu.VMEM((3, 2, ROWS, COLS), bf),
            pltpu.VMEM((COLS, 4 * COLS), bf),
            pltpu.VMEM((COLS, 4 * COLS), bf),
            pltpu.VMEM((3, 2, ROWS, COLS), f32),
            pltpu.VMEM((3, 3, ROWS, COLS), bf),
            pltpu.VMEM((3, 3, ROWS, COLS), bf),
            pltpu.VMEM((3, ROWS, COLS), bf),
            dma((8,)), dma((4,)), dma((31,)), dma((32,)), dma((3,)), dma((3,)),
            dma((4,)), dma((4,)), dma((12,)), dma((12,)),
        ],
        compiler_params=pltpu.CompilerParams(
            collective_id=0, has_side_effects=True, vmem_limit_bytes=VMEM_LIMIT
        ),
        cost_estimate=pl.CostEstimate(
            flops=20_000_000_000, bytes_accessed=16_000_000, transcendentals=32_000_000
        ),
    )(sol_q, solution_keys, solution_values, crit_q, crit_k, critique_values, boundary, w_out)
    return sol_out, crit_out


def solution(mesh):
    in_specs = (
        P("seq", "tp"), P("seq", "tp"), P("seq", "tp"),
        P("seq", None, "tp"), P("seq", None, "tp"), P("seq", None, "tp"),
        P(), P("tp", None),
    )
    out_specs = (P("seq", "tp"), P("seq", None, "tp"))
    return jax.shard_map(
        per_device, mesh=mesh, in_specs=in_specs, out_specs=out_specs, check_vma=False
    )
```

```python
import functools
import math

import jax
import jax.numpy as jnp
from jax import lax
from jax.experimental import pallas as pl
from jax.experimental.pallas import tpu as pltpu
from jax.sharding import PartitionSpec as P

HEAD = 128
HEADS = 5
ROWS = 256
WIDE = HEADS * ROWS
COLS = HEADS * HEAD
KEYS = 512
NEG = -1e30
SCALE = math.log2(math.e) / math.sqrt(HEAD)
VMEM_LIMIT = 63 * 2**20
AT = (0, 1, 4, 7, 10, 12, 14)
KV = True
ATT = True
WX = True
XX = True
PJ = True

ORDER = (
    (0, -1), (0, 1), (-1, 0), (1, 0), (0, 2), (2, 0), (-1, -1), (-1, 1),
    (1, -1), (1, 1), (-1, 2), (1, 2), (2, -1), (2, 1), (2, 2),
)
STEPS = (
    (("y", "0", "m"), ("z", "m"), ("z", "p"), ("w",), ("y", "0", "p")),
    (),
    (("y", "0", "2"),),
    (("z", "2"),),
    (),
    (("y", "m", "m"), ("y", "p", "m")),
    (("y", "m", "p"), ("y", "p", "p")),
    (),
    (("y", "2", "m"),),
    (("y", "2", "p"),),
    (("y", "m", "2"), ("y", "p", "2")),
    (("y", "2", "2"),),
    (), (), (),
)


def pick(index, table):
    value = jnp.int32(table[0])
    for at, entry in enumerate(table[1:], 1):
        value = jnp.where(index == at, jnp.int32(entry), value)
    return value


def kernel(
    sol_q_in, sol_k_in, sol_v_in, crit_q_in, crit_k_in, crit_v_in, bnd_in, w_hbm, sol_out, crit_out,
    sol_q, sol_k, sol_v, crit_q, crit_k, crit_v, bnd, kv, own_kv, sbuf, acc, top, att, wown, wpar,
    hold, msend, mrecv, done,
    in_sem, out_sem, kv_send, kv_recv, w_send, w_recv, z_send, z_recv, m_send, m_recv,
):
    s = lax.axis_index("seq")
    t = lax.axis_index("tp")
    a, b, c = s // 8, (s // 2) % 4, s % 2
    ch = s // 2
    sib = s + 1 - 2 * c
    zl, x = t // 4, t % 4
    d = 1 - 2 * c

    def seq_at(za, yb):
        return za * 8 + yb * 2 + c

    def hop(v, by):
        return (v + by + 8) % 4

    def rel(v, which):
        return {"0": v, "m": hop(v, -d), "p": hop(v, d), "2": hop(v, 2)}[which]

    def tp_at(xx):
        return zl * 4 + xx

    partner = (1 - zl) * 4 + x
    beyond = seq_at(hop(a, 2 * zl - 1), b)

    def remote(src, dst, ssem, rsem, seq=None, tp=None):
        return pltpu.make_async_remote_copy(
            src_ref=src, dst_ref=dst, send_sem=ssem, recv_sem=rsem,
            device_id={"seq": s if seq is None else seq, "tp": t if tp is None else tp},
            device_id_type=pl.DeviceIdType.MESH,
        )

    loads = [
        pltpu.make_async_copy(src, dst, in_sem.at[k])
        for k, (src, dst) in enumerate((
            (sol_k_in, sol_k), (sol_v_in, sol_v), (sol_q_in, sol_q), (crit_k_in, crit_k),
            (crit_v_in, crit_v), (crit_q_in, crit_q), (bnd_in, bnd),
            (w_hbm.at[:, pl.ds(pl.multiple_of(zl * 2560, 128), 2560)], wown),
        ))
    ]
    for load in loads:
        load.start()

    barrier = pltpu.get_barrier_semaphore()
    friends = [
        (seq_at(hop(a, 1), b), t), (seq_at(hop(a, -1), b), t),
        (seq_at(a, hop(b, 1)), t), (seq_at(a, hop(b, -1)), t), (sib, t),
    ]
    friends += [(s, tp_at(hop(x, 1))), (s, tp_at(hop(x, -1))), (s, partner), (beyond, partner)]
    for fs, ft in friends:
        pl.semaphore_signal(
            barrier, inc=1, device_id={"seq": fs, "tp": ft}, device_id_type=pl.DeviceIdType.MESH
        )
    loads[0].wait()
    loads[1].wait()
    kv[s, 0:256, :] = sol_k[...]
    kv[s, 256:384, :] = sol_v[0:128, :].T
    kv[s, 384:512, :] = sol_v[128:256, :].T
    pl.semaphore_wait(barrier, len(friends))

    sent = [0]

    def send_kv(block, to):
        if not KV:
            return
        k = sent[0]
        sent[0] += 1
        remote(kv.at[block], kv.at[block], kv_send.at[k], kv_recv.at[block], seq=to).start()

    def wait_kv(block):
        if not KV:
            return
        remote(kv.at[block], kv.at[block], kv_send.at[0], kv_recv.at[block], seq=sib).wait_recv()

    def send_y(block):
        send_kv(block, seq_at(a, hop(b, d)))
        send_kv(block, seq_at(a, hop(b, -d)))

    send_kv(s, seq_at(hop(a, d), b))
    send_kv(s, seq_at(hop(a, -d), b))
    send_y(s)
    send_kv(s, sib)

    def service(item):
        if item[0] == "w":
            w_start()
            return
        if item[0] == "z":
            block = seq_at(rel(a, item[1]), b)
            wait_kv(block)
            if item[1] == "m":
                send_kv(block, seq_at(hop(a, d), b))
            send_y(block)
            send_kv(block, sib)
        else:
            block = seq_at(rel(a, item[1]), rel(b, item[2]))
            wait_kv(block)
            if item[2] == "m":
                send_kv(block, seq_at(a, hop(b, d)))
            send_kv(block, sib)

    def w_copy(n):
        rows = pl.ds(pl.multiple_of(c * 320 + n * 160, 16), 160)
        return remote(
            w_hbm.at[rows, pl.ds(pl.multiple_of((1 - zl) * 2560, 128), 2560)],
            wpar.at[rows, :], w_send.at[n], w_recv.at[n],
            seq=(s, beyond)[n], tp=partner,
        )

    def w_start():
        if WX:
            w_copy(0).start()
            w_copy(1).start()

    def w_shared(which):
        rows = pl.ds(pl.multiple_of(which * 320, 16), 320)
        return remote(wpar.at[rows, :], wpar.at[rows, :], w_send.at[2], w_recv.at[2], seq=sib)

    def w_share():
        if WX:
            w_copy(0).wait_recv()
            w_copy(1).wait_recv()
            w_shared(c).start()

    def w_ready():
        if WX:
            w_shared(1 - c).wait_recv()
        loads[7].wait()

    def query(g, h):
        if isinstance(g, int) and g == 0:
            return sol_q[:, h * HEAD:(h + 1) * HEAD]
        return crit_q[g - 1, :, h * HEAD:(h + 1) * HEAD]

    def dot_keys(keys, g, h):
        return lax.dot_general(
            keys, query(g, h), (((1,), (1,)), ((), ())), preferred_element_type=jnp.float32
        )

    def keys_of(j):
        return kv[pl.ds(2 * j, 2), 0:256, :].reshape(KEYS, HEAD)

    def values_of(j):
        parts = [kv[2 * j, 256:384, :], kv[2 * j, 384:512, :],
                 kv[2 * j + 1, 256:384, :], kv[2 * j + 1, 384:512, :]]
        return jnp.concatenate(
            [jnp.concatenate(parts, axis=1), jnp.ones((16, KEYS), jnp.bfloat16)], axis=0
        )

    def absorb(u, h, scores, values):
        cs = slice(h * ROWS, (h + 1) * ROWS)
        old = top[u, 0:1, cs]
        new = jnp.maximum(old, jnp.max(scores, axis=0, keepdims=True))
        rescale = jnp.exp2((old - new) * SCALE)
        weights = jnp.exp2((scores - new) * SCALE).astype(jnp.bfloat16)
        acc[u, :, cs] = acc[u, :, cs] * rescale + lax.dot_general(
            values, weights, (((1,), (0,)), ((), ())), preferred_element_type=jnp.float32
        )
        top[u, 0:1, cs] = new

    def reset(unit):
        if not ATT:
            return
        u, g, v = unit
        top[u] = jnp.full((8, WIDE), NEG, jnp.float32)
        acc[u] = jnp.zeros((HEAD + 16, WIDE), jnp.float32)

    def begin(unit):
        if not ATT:
            return
        u, g, v = unit
        keys = keys_of(ch)
        key_at = lax.broadcasted_iota(jnp.int32, (KEYS, ROWS), 0)
        if g == 0:
            allowed = key_at <= lax.broadcasted_iota(jnp.int32, (KEYS, ROWS), 1) + 256 * c
        else:
            allowed = key_at < bnd[2 * s + g - 1] - KEYS * ch
        for h in range(HEADS):
            sbuf[v, h] = jnp.where(allowed, dot_keys(keys, g, h), NEG)

    def advance(units, now, then):
        if not ATT:
            return
        values, keys = values_of(now), keys_of(then)
        for h in range(HEADS):
            for u, g, v in units:
                absorb(u, h, sbuf[v, h], values)
                sbuf[v, h] = dot_keys(keys, g, h)

    def only_keys(units, then):
        if not ATT:
            return
        keys = keys_of(then)
        for h in range(HEADS):
            for u, g, v in units:
                sbuf[v, h] = dot_keys(keys, g, h)

    def last(units, now):
        if not ATT:
            return
        values = values_of(now)
        for h in range(HEADS):
            for u, g, v in units:
                absorb(u, h, sbuf[v, h], values)

    def own(unit):
        if not ATT:
            return
        u, g, v = unit
        keys = own_kv[g - 1, 0:256, :]
        values = jnp.concatenate(
            [
                jnp.concatenate([own_kv[g - 1, 256:384, :], own_kv[g - 1, 384:512, :]], axis=1),
                jnp.ones((16, 256), jnp.bfloat16),
            ],
            axis=0,
        )
        shape = (256, ROWS)
        allowed = lax.broadcasted_iota(jnp.int32, shape, 0) <= lax.broadcasted_iota(jnp.int32, shape, 1)
        for h in range(HEADS):
            sbuf[v, h, 0:256, :] = jnp.where(allowed, dot_keys(keys, g, h), NEG)
        for h in range(HEADS):
            absorb(u, h, sbuf[v, h, 0:256, :], values)

    def finish(u, g, half):
        if not ATT:
            return
        for h in range(HEADS):
            at = h * ROWS + half * HEAD
            cs = slice(at, at + HEAD)
            value = acc[u, 0:HEAD, cs] * (1.0 / acc[u, HEAD:HEAD + 1, cs])
            att[g, 0, half * HEAD:(half + 1) * HEAD, h * HEAD:(h + 1) * HEAD] = (
                value.astype(jnp.bfloat16).T
            )

    def z_copy(chunk):
        k, g, r, n = chunk
        return remote(
            att.at[g, 0, pl.ds(r, n), :], att.at[g, 1, pl.ds(r, n), :],
            z_send.at[k], z_recv.at[k], tp=partner,
        )

    def m_copy(chunk, kind, to):
        k, g, r, n = chunk
        return remote(
            msend.at[g, kind, pl.ds(r, n), :], mrecv.at[g, kind, pl.ds(r, n), :],
            m_send.at[3 * k + kind], m_recv.at[3 * k + kind], tp=tp_at(to),
        )

    def z_start(chunk):
        if XX:
            z_copy(chunk).start()

    def project(chunk):
        k, g, r, n = chunk
        if XX:
            z_copy(chunk).wait_recv()

        def part(at):
            cols = pl.ds(pl.multiple_of(at * COLS, 128), COLS)
            if not PJ:
                return jnp.zeros((n, COLS), jnp.float32)
            return jnp.dot(
                att[g, 0, r:r + n, :], wown[:, cols], preferred_element_type=jnp.float32
            ) + jnp.dot(att[g, 1, r:r + n, :], wpar[:, cols], preferred_element_type=jnp.float32)

        for kind, at, to in ((0, hop(x, 2), hop(x, d)), (1, hop(x, -d), hop(x, -d))):
            msend[g, kind, r:r + n, :] = part(at).astype(jnp.bfloat16)
            if XX:
                m_copy(chunk, kind, to).start()
        hold[g, 0, r:r + n, :] = part(hop(x, d))
        hold[g, 1, r:r + n, :] = part(x)

    def relay(chunk):
        k, g, r, n = chunk
        if XX:
            m_copy(chunk, 0, hop(x, d)).wait_recv()
        total = hold[g, 0, r:r + n, :] + mrecv[g, 0, r:r + n, :].astype(jnp.float32)
        msend[g, 2, r:r + n, :] = total.astype(jnp.bfloat16)
        if XX:
            m_copy(chunk, 2, hop(x, d)).start()

    def store(chunk):
        k, g, r, n = chunk
        rows = pl.ds(r, n)
        ref = sol_out.at[rows, :] if g == 0 else crit_out.at[g - 1, rows, :]
        return pltpu.make_async_copy(done.at[g, rows, :], ref, out_sem.at[k])

    def complete(chunk):
        k, g, r, n = chunk
        total = hold[g, 1, r:r + n, :]
        for kind in (1, 2):
            if XX:
                m_copy(chunk, kind, hop(x, d)).wait_recv()
            total += mrecv[g, kind, r:r + n, :].astype(jnp.float32)
        done[g, r:r + n, :] = total.astype(jnp.bfloat16)
        store(chunk).start()

    chunks = (
        (0, 0, 0, 128), (1, 0, 128, 128), (2, 1, 0, 256), (3, 2, 0, 128), (4, 2, 128, 128)
    )

    first = ((0, 0, 0), (1, 1, 1))
    second = ((2, 2, 0),)
    for unit in first + second:
        reset(unit)
    for k in (2, 3, 4, 5, 6):
        loads[k].wait()
    for i in range(2):
        own_kv[i, 0:256, :] = crit_k[i]
        own_kv[i, 256:384, :] = crit_v[i, 0:128, :].T
        own_kv[i, 384:512, :] = crit_v[i, 128:256, :].T
    own(first[1])
    own(second[0])
    wait_kv(sib)
    begin(second[0])
    last(second, ch)
    begin(first[0])
    begin(first[1])

    def slot(e, carry):
        before, before_ok = carry
        for at, items in enumerate(STEPS):
            if items:
                @pl.when(e == at)
                def _(items=items):
                    for item in items:
                        service(item)
        j = hop(a, pick(e, [o[0] for o in ORDER])) * 4 + hop(b, pick(e, [o[1] for o in ORDER]))
        wait_kv(2 * j + 1 - c)
        ok = j < ch

        @pl.when(before_ok)
        def _():
            advance(first, before, j)

        @pl.when(jnp.logical_and(jnp.logical_not(before_ok), ok))
        def _():
            only_keys(first, j)

        return j, ok

    before, before_ok = lax.fori_loop(0, 15, slot, (ch, jnp.bool_(True)))

    @pl.when(before_ok)
    def _():
        last(first, before)

    for half in range(2):
        finish(0, 0, half)
        z_start(chunks[half])
    finish(1, 1, 0)
    finish(1, 1, 1)

    @pl.when(ch > 0)
    def _():
        only_keys(second, 0)


    def step(i, _):
        for at, work in (
            (AT[0], w_share),
            (AT[1], lambda: z_start(chunks[2])),
            (AT[2], lambda: (w_ready(), project(chunks[0]))),
            (AT[3], lambda: project(chunks[1])),
            (AT[4], lambda: relay(chunks[0])),
            (AT[5], lambda: project(chunks[2])),
            (AT[6], lambda: relay(chunks[1])),
        ):
            @pl.when(i == at)
            def _(work=work):
                work()

        @pl.when(i < ch - 1)
        def _():
            advance(second, i, i + 1)

        return 0

    lax.fori_loop(0, 15, step, 0)

    @pl.when(ch > 0)
    def _():
        last(second, ch - 1)

    for half in range(2):
        finish(2, 2, half)
        z_start(chunks[3 + half])
    relay(chunks[2])
    complete(chunks[0])
    complete(chunks[1])
    project(chunks[3])
    project(chunks[4])
    relay(chunks[3])
    complete(chunks[2])
    relay(chunks[4])
    complete(chunks[3])
    complete(chunks[4])

    for k in range(sent[0]):
        remote(kv.at[0], kv.at[0], kv_send.at[k], kv_recv.at[0], seq=sib).wait_send()
    if WX:
        w_copy(0).wait_send()
        w_copy(1).wait_send()
        w_shared(c).wait_send()
    for chunk in chunks:
        if XX:
            z_copy(chunk).wait_send()
            for kind in range(3):
                m_copy(chunk, kind, hop(x, d)).wait_send()
        store(chunk).wait()


def per_device(
    sol_q, solution_keys, solution_values, crit_q, crit_k, critique_values, boundary, w_out
):
    bf, f32 = jnp.bfloat16, jnp.float32
    dma = pltpu.SemaphoreType.DMA
    hbm = pl.BlockSpec(memory_space=pl.ANY)
    sol_out, crit_out = pl.pallas_call(
        kernel,
        out_shape=(
            jax.ShapeDtypeStruct((ROWS, COLS), bf), jax.ShapeDtypeStruct((2, ROWS, COLS), bf)
        ),
        in_specs=[hbm] * 8,
        out_specs=(hbm, hbm),
        scratch_shapes=[
            pltpu.VMEM((ROWS, COLS), bf),
            pltpu.VMEM((ROWS, HEAD), bf),
            pltpu.VMEM((ROWS, HEAD), bf),
            pltpu.VMEM((2, ROWS, COLS), bf),
            pltpu.VMEM((2, ROWS, HEAD), bf),
            pltpu.VMEM((2, ROWS, HEAD), bf),
            pltpu.SMEM((64,), jnp.int32),
            pltpu.VMEM((32, 512, HEAD), bf),
            pltpu.VMEM((2, 512, HEAD), bf),
            pltpu.VMEM((2, HEADS, KEYS, ROWS), f32),
            pltpu.VMEM((3, HEAD + 16, WIDE), f32),
            pltpu.VMEM((3, 8, WIDE), f32),
            pltpu.VMEM((3, 2, ROWS, COLS), bf),
            pltpu.VMEM((COLS, 4 * COLS), bf),
            pltpu.VMEM((COLS, 4 * COLS), bf),
            pltpu.VMEM((3, 2, ROWS, COLS), f32),
            pltpu.VMEM((3, 3, ROWS, COLS), bf),
            pltpu.VMEM((3, 3, ROWS, COLS), bf),
            pltpu.VMEM((3, ROWS, COLS), bf),
            dma((8,)), dma((5,)), dma((31,)), dma((32,)), dma((3,)), dma((3,)),
            dma((5,)), dma((5,)), dma((15,)), dma((15,)),
        ],
        compiler_params=pltpu.CompilerParams(
            collective_id=0, has_side_effects=True, vmem_limit_bytes=VMEM_LIMIT
        ),
        cost_estimate=pl.CostEstimate(
            flops=20_000_000_000, bytes_accessed=16_000_000, transcendentals=32_000_000
        ),
    )(sol_q, solution_keys, solution_values, crit_q, crit_k, critique_values, boundary, w_out)
    return sol_out, crit_out


def solution(mesh):
    in_specs = (
        P("seq", "tp"), P("seq", "tp"), P("seq", "tp"),
        P("seq", None, "tp"), P("seq", None, "tp"), P("seq", None, "tp"),
        P(), P("tp", None),
    )
    out_specs = (P("seq", "tp"), P("seq", None, "tp"))
    return jax.shard_map(
        per_device, mesh=mesh, in_specs=in_specs, out_specs=out_specs, check_vma=False
    )
```
